128 devices in a mesh: rep: 8 (over y_lo, x), fsdp: 16 (over y_hi, z, core).
Axes of the slice: x: 4, y: 4 (y_hi: 2, y_lo: 2; y = y_hi * 2 + y_lo), z: 4, core: 2. Of those that a mesh axis runs over, the one named last changes fastest.
Arguments:
- inputs: bfloat16 [8, 8192, 8192], P('rep', 'fsdp'), may hold values from -6 to 6
- grad_keys: bfloat16 [8, 8192, 1024], P('rep', 'fsdp'), may hold values from -1.5 to 1.5
- local_weights: bfloat16 [8, 8192, 1024], P('rep', 'fsdp'), may hold values from -6 to 6
- feedback: bfloat16 [8, 8192, 1024], P('rep', 'fsdp'), may hold values from -4 to 4
- base: float32 [8192, 1024], P('fsdp', 'rep'), may hold values from -6 to 6
- momentum: float32 [8192, 1024], P('fsdp', 'rep'), may hold values from -4 to 4
- warm_start: float32 [1024, 64], replicated, may hold values from -6 to 6
Outputs:
- grad_inputs: bfloat16 [8, 8192, 8192], P('rep', 'fsdp')
- feedback_out: float32 [8, 8192, 1024], P('rep', 'fsdp')
- base_out: float32 [8192, 1024], P('fsdp', 'rep')
- momentum_out: float32 [8192, 1024], P('fsdp', 'rep')
- factor_out: float32 [1024, 64], replicated
The draws below stay inside these ranges and needn't reach their ends.
All inputs are finite; a program needn't handle non-finite values.
Results may differ from the reference program's by a relative error of at most 0.0018.
Values may be sent and summed in bfloat16 or wider, within the bound.
No kernel may reach another device: no remote copies, remote signals or barrier semaphores. Data moves between devices by JAX's collectives and lax.ppermute only.
A program may use at most 128 MiB of HBM per device.

```python
import jax
import jax.numpy as jnp
from jax import lax

D = 8192
KV = 1024
RANK = 64
ROUNDS = 2
TOK_DEV = 512
TOKR = 8192
N_REP = 8
N_FSDP = 16


def with_spikes(result, rng, source, target, blocks, factor):
    owner, partner = [(jnp.arange(result.shape[dim]) // (result.shape[dim] // blocks)).reshape([-1 if axis == dim else 1 for axis in range(result.ndim)]) for dim in (source, target)]
    chosen = jax.random.permutation(rng, blocks)[partner]
    strong = (owner == chosen) | (owner == (partner + blocks // 2) % blocks)
    return jnp.where(strong, factor * result, result)


def block_scale(stream_key, extent, pieces, smallest, high):
    def one(axis_at, blocks):
        heights = jax.random.uniform(jax.random.fold_in(jax.random.fold_in(stream_key, 6), axis_at), (blocks,), jnp.float32, smallest / len(pieces), high / len(pieces))
        return jnp.repeat(jnp.exp(heights), extent[axis_at] // blocks).reshape((-1,) + (1,) * (len(extent) - axis_at - 1))

    factor_of = one(*pieces[0])
    for cut in pieces[1:]:
        factor_of = factor_of * one(*cut)
    return factor_of


def scatter_about(rng, extent, deviation, reach, shards=(), kind=jnp.bfloat16):
    factor_of = block_scale(rng, extent, shards, -0.22, 0.18) if shards else 1.0
    entries = jax.random.normal(rng, extent, jnp.float32) * deviation * factor_of
    return jnp.minimum(jnp.maximum(entries, -reach), reach).astype(kind)


def noise_with(rng, dims, width, bound, pieces, heavy, kind=jnp.bfloat16):
    values = width * jax.random.normal(rng, dims, jnp.float32)
    if pieces:
        values = values * block_scale(rng, dims, pieces, -0.22, 0.18)
    return jnp.clip(with_spikes(values, jax.random.fold_in(rng, 3), *heavy), -bound, bound).astype(kind)


def setup_inputs(seed: int = 0) -> dict:
    seeds = jax.random.split(jax.random.key(seed), 8)
    return {
        "inputs": noise_with(seeds[0], (N_REP, TOKR, D), 1.0, 6.0, ((0, 8), (1, 16)), (1, 2, 16, 2.0)),
        "grad_keys": scatter_about(seeds[1], (N_REP, TOKR, KV), 0.25, 1.5, ((0, 8), (1, 16))),
        "local_weights": scatter_about(seeds[2], (N_REP, D, KV), 1.0, 6.0, ((0, 8), (1, 16))),
        "feedback": scatter_about(seeds[3], (N_REP, D, KV), 0.5, 4.0, ((0, 8), (1, 16))),
        "base": scatter_about(seeds[4], (D, KV), 1.0, 6.0, ((0, 16), (1, 8)), jnp.float32),
        "momentum": scatter_about(seeds[5], (D, KV), 0.5, 4.0, ((0, 16), (1, 8)), jnp.float32),
        "warm_start": scatter_about(seeds[6], (KV, RANK), 1.0, 6.0, (), jnp.float32),
    }


outer_rate = 0.7
momentum_keep = 0.9
inner_rate = 0.5

def orthonormal_part(matrix, lower_factor):
    return lax.linalg.triangular_solve(lower_factor, matrix, left_side=False, lower=True, transpose_a=True)

def replica_step(operands):
    tokens_in, cotangent, weights = operands
    inv_root = 1.0 / jnp.sqrt(jnp.float32(D))
    grad_in = (jnp.dot(cotangent.astype(jnp.float32), weights.T.astype(jnp.float32), preferred_element_type=jnp.float32) * inv_root).astype(jnp.bfloat16)
    token_blocks = tokens_in.reshape(N_FSDP, TOK_DEV, D)
    key_blocks = cotangent.reshape(N_FSDP, TOK_DEV, KV)

    def add_block(summed, block_pair):
        term = (jnp.dot(block_pair[0].T.astype(jnp.float32), block_pair[1].astype(jnp.float32), preferred_element_type=jnp.float32) * inv_root).astype(jnp.bfloat16)
        term = lax.optimization_barrier(term)
        return (summed + term.astype(jnp.float32), None)
    summed, unused = lax.scan(add_block, jnp.zeros((D, KV), jnp.float32), (token_blocks, key_blocks))
    return (grad_in, summed)

def reference(inputs, grad_keys, local_weights, feedback, base, momentum, warm_start):
    highest = lax.Precision.HIGHEST
    grad_inputs, inner_grad = lax.map(replica_step, (inputs, grad_keys, local_weights))
    pseudo = base[None] - local_weights.astype(jnp.float32) + inner_rate * inner_grad + feedback.astype(jnp.float32)
    factor = warm_start
    orthonormal = None
    for repeat in range(ROUNDS):
        left_part = jnp.einsum('rdk,kq->dq', pseudo, factor, precision=highest) / N_REP
        gram_matrix = jnp.dot(left_part.T, left_part, precision=highest)
        lower_factor = jnp.linalg.cholesky(gram_matrix)
        orthonormal = orthonormal_part(left_part, lower_factor)
        factor = jnp.einsum('rdk,dq->kq', pseudo, orthonormal, precision=highest) / N_REP
    approx = jnp.dot(orthonormal, factor.T, precision=highest)
    feedback_out = pseudo - approx[None]
    momentum_out = momentum_keep * momentum + approx
    base_out = base - outer_rate * (approx + momentum_keep * momentum_out)
    return (grad_inputs, feedback_out, base_out, momentum_out, factor)
```

```python
import math

import jax
import jax.numpy as jnp
from jax import lax
from jax.sharding import Mesh, PartitionSpec as P

D = 8192
ROUNDS = 2

outer_rate = 0.7
momentum_keep = 0.9
inner_rate = 0.5

REP = ("yl", "x")
FSDP = ("yh", "z", "c")
CHIPS = ("yh", "z")
ALL = REP + FSDP
f32 = jnp.float32
bf16 = jnp.bfloat16


def dot(a, b, dims=((1,), (0,))):
    return lax.dot_general(
        a, b, (dims, ((), ())), precision=lax.Precision.HIGHEST, preferred_element_type=f32
    )


def scatter_sum(value, axes, parts):
    got = lax.all_to_all(value, axes, 0, 0, tiled=True)
    return got.reshape(parts, -1, value.shape[1]).astype(f32).sum(0)


def gather_rows(value, axes, parts):
    rows, width = value.shape
    sent = jnp.broadcast_to(value[None], (parts, rows, width)).reshape(parts * rows, width)
    return lax.all_to_all(sent, axes, 0, 0, tiled=True)


def orthonormal_part(matrix, lower_factor):
    return lax.linalg.triangular_solve(
        lower_factor, matrix, left_side=False, lower=True, transpose_a=True
    )


def per_device(inputs, grad_keys, local_weights, feedback, base, momentum, warm_start):
    inv_root = 1.0 / math.sqrt(D)
    tokens_in = inputs[0]
    cotangent = grad_keys[0]
    weights = local_weights[0]
    rep_size, fsdp_size, chip_size = lax.axis_size(REP), lax.axis_size(FSDP), lax.axis_size(CHIPS)
    everyone = rep_size * fsdp_size
    core = lax.axis_index("c")
    rows, width = weights.shape

    product = lax.dot_general(
        tokens_in, cotangent, (((0,), (0,)), ((), ())), preferred_element_type=f32
    )
    term = (product * inv_root).astype(bf16).reshape(chip_size, 2, rows, width)
    away = lax.dynamic_index_in_dim(term, 1 - core, 1, keepdims=False)
    kept = lax.dynamic_index_in_dim(term, core, 1, keepdims=False)
    came = lax.ppermute(away, "c", [(0, 1), (1, 0)])
    pair = (kept.astype(f32) + came.astype(f32)).astype(bf16).reshape(chip_size * rows, width)
    inner_grad = scatter_sum(pair, CHIPS, chip_size)

    full_base = lax.all_gather(base, REP, axis=1, tiled=True)
    drift = feedback[0].astype(f32) - weights.astype(f32)
    part_rows = rows // rep_size
    my_rep = lax.axis_index(REP)
    base_part = lax.dynamic_slice_in_dim(full_base, my_rep * part_rows, part_rows, 0)
    early_mean = base_part + scatter_sum(drift, REP, rep_size) / rep_size
    pseudo_mean = early_mean + (inner_rate / rep_size) * scatter_sum(
        inner_grad.astype(bf16), REP, rep_size
    )
    pseudo = full_base + drift + inner_rate * inner_grad

    factor = warm_start
    rank = factor.shape[1]
    for repeat in range(ROUNDS):
        left_part = dot(pseudo_mean, factor)
        raised = dot(pseudo_mean, left_part, ((0,), (0,)))
        gram_part = dot(left_part, left_part, ((0,), (0,)))
        packed = jnp.concatenate(
            [raised, jnp.tile(gram_part, (raised.shape[0] // rank, 1))], axis=1
        )
        summed = gather_rows(scatter_sum(packed, ALL, everyone), ALL, everyone)
        lower_factor = jnp.linalg.cholesky(summed[:rank, rank:])
        factor = orthonormal_part(summed[:, :rank], lower_factor)
    left = gather_rows(left_part, REP, rep_size)
    orthonormal = orthonormal_part(left, lower_factor)

    approx = dot(orthonormal, factor, ((1,), (1,)))
    feedback_out = (pseudo - approx)[None]
    block_width = base.shape[1]
    column_block = lax.dynamic_slice_in_dim(approx, my_rep * block_width, block_width, 1)
    momentum_out = momentum_keep * momentum + column_block
    base_out = base - outer_rate * (column_block + momentum_keep * momentum_out)

    every_row = lax.all_gather(local_weights, FSDP, axis=1, tiled=True)[0]
    product = lax.dot_general(
        cotangent, every_row, (((1,), (1,)), ((), ())), preferred_element_type=f32
    )
    grad_inputs = (product * inv_root).astype(bf16)[None]
    return (grad_inputs, feedback_out, base_out, momentum_out, factor)


def solution(mesh):
    fine = Mesh(mesh.devices.reshape(2, 4, 2, 4, 2), ALL)
    return jax.shard_map(
        per_device,
        mesh=fine,
        in_specs=(
            P(REP, FSDP, None),
            P(REP, FSDP, None),
            P(REP, FSDP, None),
            P(REP, FSDP, None),
            P(FSDP, REP),
            P(FSDP, REP),
            P(),
        ),
        out_specs=(
            P(REP, FSDP, None),
            P(REP, FSDP, None),
            P(FSDP, REP),
            P(FSDP, REP),
            P(),
        ),
        check_vma=False,
    )
```

```python
import functools
import math

import jax
import jax.numpy as jnp
from jax import lax
from jax.experimental import pallas as pl
from jax.experimental.pallas import tpu as pltpu
from jax.sharding import PartitionSpec as P

D = 8192
ROUNDS = 2

outer_rate = 0.7
momentum_keep = 0.9
inner_rate = 0.5
inv_root = 1.0 / math.sqrt(D)

f32 = jnp.float32
bf16 = jnp.bfloat16

NZ = 4
PLACES = [(y, z, c) for y in range(2) for z in range(NZ) for c in range(2)]


def place(y, z, c):
    return ((y % 2) * NZ + z % NZ) * 2 + c % 2


def hop(value, dy=0, dz=0, dc=0):
    pairs = [(place(y, z, c), place(y + dy, z + dz, c + dc)) for y, z, c in PLACES]
    return lax.ppermute(value, "fsdp", pairs)


def dot(a, b, dims=((1,), (0,))):
    return lax.dot_general(
        a, b, (dims, ((), ())), precision=lax.Precision.HIGHEST, preferred_element_type=f32
    )


def scatter_sum(value, axes, parts):
    got = lax.all_to_all(value, axes, 0, 0, tiled=True)
    return got.reshape(parts, -1, value.shape[1]).astype(f32).sum(0)


def gather_rows(value, axes, parts):
    rows, width = value.shape
    sent = jnp.broadcast_to(value[None], (parts, rows, width)).reshape(parts * rows, width)
    return lax.all_to_all(sent, axes, 0, 0, tiled=True)


def orthonormal_part(matrix, lower_factor):
    return lax.linalg.triangular_solve(
        lower_factor, matrix, left_side=False, lower=True, transpose_a=True
    )


def term_kernel(separate, spots, halves, tokens, cotangent, *refs):
    term = inv_root * lax.dot_general(
        tokens[...], cotangent[...], (((0,), (0,)), ((), ())), preferred_element_type=f32
    )
    if not separate:
        refs[0][0] = term.astype(bf16)
        return
    total = (term + refs[0][0].astype(f32)).astype(bf16)
    for index, out in enumerate(refs[1:]):

        @pl.when(pl.program_id(0) == index)
        def _():
            out[...] = total


def term_blocks(tokens_in, cotangent, blocks, core, came=None):
    depth, wide = tokens_in.shape
    rows = wide // len(PLACES)
    half = cotangent.shape[1] // 2
    count = len(blocks)
    me = lax.axis_index("fsdp")
    y, z = me // (2 * NZ), (me // 2) % NZ
    spots = jnp.stack([place(y + dy, z + dz, core) for dy, dz, _ in blocks]).astype(jnp.int32)
    halves = jnp.array([h for _, _, h in blocks], jnp.int32)
    in_specs = [
        pl.BlockSpec((depth, rows), lambda i, spots, halves: (0, spots[i])),
        pl.BlockSpec((depth, half), lambda i, spots, halves: (0, halves[i])),
    ]
    operands = [tokens_in, cotangent]
    if came is None:
        out_specs = pl.BlockSpec((1, rows, half), lambda i, spots, halves: (i, 0, 0))
        out_shape = jax.ShapeDtypeStruct((count, rows, half), bf16)
    else:
        in_specs.append(pl.BlockSpec((1, rows, half), lambda i, spots, halves: (i, 0, 0)))
        operands.append(came)
        out_specs = [pl.BlockSpec((rows, half), lambda i, spots, halves: (0, 0))] * count
        out_shape = [jax.ShapeDtypeStruct((rows, half), bf16)] * count
    return pl.pallas_call(
        functools.partial(term_kernel, came is not None),
        grid_spec=pltpu.PrefetchScalarGridSpec(
            num_scalar_prefetch=2, grid=(count,), in_specs=in_specs, out_specs=out_specs
        ),
        out_shape=out_shape,
        compiler_params=pltpu.CompilerParams(vmem_limit_bytes=40 << 20),
        cost_estimate=pl.CostEstimate(
            flops=2 * count * depth * rows * half,
            bytes_accessed=2 * count * (depth * rows + 2 * rows * half),
            transcendentals=0,
        ),
    )(spots, halves, *operands)


def add(*values):
    total = values[0].astype(f32)
    for value in values[1:]:
        total = total + value.astype(f32)
    return total


def ring_sum(two_up, two_down, up_up, up_down, down_up, down_down, own):
    from_below = hop(two_up, dz=1)
    from_above = hop(two_down, dz=-1)
    plain_below = hop(up_down, dz=1)
    plain_above = hop(down_up, dz=-1)
    merged_below = hop(add(up_up, from_below).astype(bf16), dz=1)
    merged_above = hop(add(down_down, from_above).astype(bf16), dz=-1)
    first = add(own[0], merged_below, plain_above)
    second = add(own[1], plain_below, merged_above)
    return first, second


def reduce_terms(tokens_in, cotangent):
    core = lax.axis_index("fsdp") % 2
    groups = [
        [(1, 2, 1), (1, 1, 1), (1, 3, 1), (1, 0, 1)],
        [(0, 2, 0), (1, 2, 0), (0, 1, 0), (1, 1, 0), (0, 3, 0), (1, 3, 0)],
        [(0, 2, 1), (0, 1, 1), (0, 3, 1), (0, 0, 1), (0, 0, 0), (1, 0, 0)],
    ]
    pair = {}
    for blocks in groups:
        came = hop(term_blocks(tokens_in, cotangent, blocks, 1 - core), dc=1)
        pair.update(zip(blocks, term_blocks(tokens_in, cotangent, blocks, core, came)))
    half_rows = pair[0, 0, 1].shape[0] // 2
    both = {}
    for dz in (2, 1, 3, 0):
        got = hop(pair[1, dz, 1], dy=1)
        mine = pair[0, dz, 1]
        both[dz] = [
            add(mine[:half_rows], got[:half_rows]),
            add(mine[half_rows:], got[half_rows:]),
        ]
    near, far = ring_sum(
        pair[0, 2, 0], pair[1, 2, 0], pair[0, 1, 0], pair[1, 1, 0], pair[0, 3, 0], pair[1, 3, 0],
        (pair[0, 0, 0], pair[1, 0, 0]),
    )
    first_half = add(near, hop(far.astype(bf16), dy=1))
    both = {dz: both[dz] if dz == 0 else [v.astype(bf16) for v in both[dz]] for dz in both}
    second_half = jnp.concatenate(
        ring_sum(both[2][0], both[2][1], both[1][0], both[1][1], both[3][0], both[3][1], both[0])
    )
    return first_half, second_half


def per_device(inputs, grad_keys, local_weights, feedback, base, momentum, warm_start):
    tokens_in = inputs[0]
    cotangent = grad_keys[0]
    weights = local_weights[0]
    rep_size, fsdp_size = lax.axis_size("rep"), lax.axis_size("fsdp")
    everyone = rep_size * fsdp_size
    rows, width = weights.shape
    my_rep = lax.axis_index("rep")

    full_base = lax.all_gather(base, "rep", axis=1, tiled=True)
    drift = feedback[0].astype(f32) - weights.astype(f32)
    part_rows = rows // rep_size
    base_part = lax.dynamic_slice_in_dim(full_base, my_rep * part_rows, part_rows, 0)
    early_mean = base_part + scatter_sum(drift, "rep", rep_size) / rep_size

    halves = reduce_terms(tokens_in, cotangent)
    inner_mean = jnp.concatenate(
        [scatter_sum(half.astype(bf16), "rep", rep_size) for half in halves], axis=1
    )
    pseudo_mean = early_mean + (inner_rate / rep_size) * inner_mean
    pseudo = full_base + drift + inner_rate * jnp.concatenate(halves, axis=1)

    late_weights, pseudo = lax.optimization_barrier((local_weights, pseudo))
    every_row = lax.all_gather(late_weights, "fsdp", axis=1, tiled=True)[0]

    factor = warm_start
    rank = factor.shape[1]
    everything = ("rep", "fsdp")
    for repeat in range(ROUNDS):
        left_part = dot(pseudo_mean, factor)
        raised = dot(pseudo_mean, left_part, ((0,), (0,)))
        gram_part = dot(left_part, left_part, ((0,), (0,)))
        packed = jnp.concatenate(
            [raised, jnp.tile(gram_part, (raised.shape[0] // rank, 1))], axis=1
        )
        summed = gather_rows(scatter_sum(packed, everything, everyone), everything, everyone)
        lower_factor = jnp.linalg.cholesky(summed[:rank, rank:])
        factor = orthonormal_part(summed[:, :rank], lower_factor)
    left = gather_rows(left_part, "rep", rep_size)
    orthonormal = orthonormal_part(left, lower_factor)

    approx = dot(orthonormal, factor, ((1,), (1,)))
    feedback_out = (pseudo - approx)[None]
    block_width = base.shape[1]
    column_block = lax.dynamic_slice_in_dim(approx, my_rep * block_width, block_width, 1)
    momentum_out = momentum_keep * momentum + column_block
    base_out = base - outer_rate * (column_block + momentum_keep * momentum_out)

    product = lax.dot_general(
        cotangent, every_row, (((1,), (1,)), ((), ())), preferred_element_type=f32
    )
    grad_inputs = (product * inv_root).astype(bf16)[None]
    return (grad_inputs, feedback_out, base_out, momentum_out, factor)


def solution(mesh):
    split = P("rep", "fsdp", None)
    shared = P("fsdp", "rep")
    return jax.shard_map(
        per_device,
        mesh=mesh,
        in_specs=(split, split, split, split, shared, shared, P()),
        out_specs=(split, split, shared, shared, P()),
        check_vma=False,
    )
```

```python
import functools
import math

import jax
import jax.numpy as jnp
from jax import lax
from jax.experimental import pallas as pl
from jax.experimental.pallas import tpu as pltpu
from jax.sharding import PartitionSpec as P

D = 8192
ROUNDS = 2

outer_rate = 0.7
momentum_keep = 0.9
inner_rate = 0.5
inv_root = 1.0 / math.sqrt(D)

f32 = jnp.float32
bf16 = jnp.bfloat16

NZ = 4
FIRST = 640
PLACES = [(y, z, c) for y in range(2) for z in range(NZ) for c in range(2)]


def place(y, z, c):
    return ((y % 2) * NZ + z % NZ) * 2 + c % 2


def hop(value, dy=0, dz=0, dc=0):
    pairs = [(place(y, z, c), place(y + dy, z + dz, c + dc)) for y, z, c in PLACES]
    return lax.ppermute(value, "fsdp", pairs)


def dot(a, b, dims=((1,), (0,))):
    return lax.dot_general(
        a, b, (dims, ((), ())), precision=lax.Precision.HIGHEST, preferred_element_type=f32
    )


def scatter_sum(value, axes, parts):
    got = lax.all_to_all(value, axes, 0, 0, tiled=True)
    return got.reshape(parts, -1, value.shape[1]).astype(f32).sum(0)


def gather_rows(value, axes, parts):
    rows, width = value.shape
    sent = jnp.broadcast_to(value[None], (parts, rows, width)).reshape(parts * rows, width)
    return lax.all_to_all(sent, axes, 0, 0, tiled=True)


def orthonormal_part(matrix, lower_factor):
    return lax.linalg.triangular_solve(
        lower_factor, matrix, left_side=False, lower=True, transpose_a=True
    )


def after(value, *others):
    return lax.optimization_barrier((value,) + others)[0]


def term_kernel(separate, spots, tokens, cotangent, *refs):
    term = inv_root * lax.dot_general(
        tokens[...], cotangent[...], (((0,), (0,)), ((), ())), preferred_element_type=f32
    )
    if not separate:
        refs[0][0] = term.astype(bf16)
        return
    total = (term + refs[0][0].astype(f32)).astype(bf16)
    if len(refs) == 2:
        refs[1][0] = total
        return
    for index, out in enumerate(refs[1:]):

        @pl.when(pl.program_id(0) == index)
        def _():
            out[...] = total


def term_blocks(tokens_in, cotangent, blocks, core, came=None, stacked=False):
    depth, wide = tokens_in.shape
    rows = wide // len(PLACES)
    width = cotangent.shape[1]
    count = len(blocks)
    me = lax.axis_index("fsdp")
    y, z = me // (2 * NZ), (me // 2) % NZ
    spots = jnp.stack([place(y + dy, z + dz, core) for dy, dz in blocks]).astype(jnp.int32)
    one = pl.BlockSpec((1, rows, width), lambda i, spots: (i, 0, 0))
    in_specs = [
        pl.BlockSpec((depth, rows), lambda i, spots: (0, spots[i])),
        pl.BlockSpec((depth, width), lambda i, spots: (0, 0)),
    ]
    operands = [tokens_in, cotangent]
    out_specs = one
    out_shape = jax.ShapeDtypeStruct((count, rows, width), bf16)
    if came is not None:
        in_specs.append(one)
        operands.append(came)
        if not stacked:
            out_specs = [pl.BlockSpec((rows, width), lambda i, spots: (0, 0))] * count
            out_shape = [jax.ShapeDtypeStruct((rows, width), bf16)] * count
    return pl.pallas_call(
        functools.partial(term_kernel, came is not None),
        grid_spec=pltpu.PrefetchScalarGridSpec(
            num_scalar_prefetch=1, grid=(count,), in_specs=in_specs, out_specs=out_specs
        ),
        out_shape=out_shape,
        compiler_params=pltpu.CompilerParams(vmem_limit_bytes=40 << 20),
        cost_estimate=pl.CostEstimate(
            flops=2 * count * depth * rows * width,
            bytes_accessed=2 * count * (depth * rows + 2 * rows * width),
            transcendentals=0,
        ),
    )(spots, *operands)


def grad_kernel(firsts, spots, cotangent, *refs):
    out = refs[-1]
    for index, first in enumerate(firsts):
        block = refs[index]
        here = pl.program_id(0)

        @pl.when((here >= first) & (here < first + block_count(firsts, index, spots)))
        def _():
            product = lax.dot_general(
                cotangent[...], block[0], (((1,), (1,)), ((), ())), preferred_element_type=f32
            )
            out[...] = (inv_root * product).astype(bf16)


def block_count(firsts, index, spots):
    last = spots.shape[0] if index + 1 == len(firsts) else firsts[index + 1]
    return last - firsts[index]


def grad_blocks(cotangent, stacks, places, wide, before=None):
    tokens, depth = cotangent.shape
    rows = stacks[0].shape[1]
    counts = [stack.shape[0] for stack in stacks]
    firsts = [sum(counts[:i]) for i in range(len(counts))]
    total = sum(counts)
    spots = jnp.stack(places).astype(jnp.int32)

    def chosen(first, count):
        return lambda i, spots: (jnp.clip(i - first, 0, count - 1), 0, 0)

    in_specs = [pl.BlockSpec((tokens, depth), lambda i, spots: (0, 0))]
    in_specs += [
        pl.BlockSpec((1, rows, depth), chosen(first, count))
        for first, count in zip(firsts, counts)
    ]
    operands = [cotangent, *stacks]
    aliases = {}
    if before is not None:
        in_specs.append(pl.BlockSpec(memory_space=pl.ANY))
        operands.append(before)
        aliases = {len(operands): 0}
    return pl.pallas_call(
        functools.partial(grad_kernel, firsts),
        grid_spec=pltpu.PrefetchScalarGridSpec(
            num_scalar_prefetch=1,
            grid=(total,),
            in_specs=in_specs,
            out_specs=pl.BlockSpec((tokens, rows), lambda i, spots: (0, spots[i])),
        ),
        out_shape=jax.ShapeDtypeStruct((tokens, wide), bf16),
        input_output_aliases=aliases,
        compiler_params=pltpu.CompilerParams(vmem_limit_bytes=40 << 20),
        cost_estimate=pl.CostEstimate(
            flops=2 * total * tokens * depth * rows,
            bytes_accessed=2 * total * rows * (depth + tokens),
            transcendentals=0,
        ),
    )(spots, *operands)


def add(*values):
    total = values[0].astype(f32)
    for value in values[1:]:
        total = total + value.astype(f32)
    return total


def reduce_terms(tokens_in, cotangent, early):
    core = lax.axis_index("fsdp") % 2
    other = 1 - core
    first_part, second_part = cotangent[:, :FIRST], cotangent[:, FIRST:]
    far, near, own = [(0, 2), (1, 2)], [(0, 1), (1, 1), (0, 3), (1, 3)], [(0, 0), (1, 0)]
    cross = [(1, 2), (1, 1), (1, 3), (1, 0)]
    straight = [(0, 2), (0, 1), (0, 3), (0, 0)]

    away_far = term_blocks(tokens_in, first_part, far, other)
    came_far = hop(away_far, dc=1)
    away_near = term_blocks(tokens_in, after(first_part, away_far), near, other)
    came_near = hop(away_near, dc=1)
    far_y0, far_y1 = term_blocks(tokens_in, after(first_part, away_near), far, core, came_far)
    below = hop(far_y0, dz=1)
    above = hop(far_y1, dz=-1)
    away_second = term_blocks(tokens_in, after(second_part, far_y0), cross + straight, other)
    came_second = hop(away_second, dc=1)
    up_y0, up_y1, down_y0, down_y1 = term_blocks(
        tokens_in, after(first_part, away_second), near, core, came_near
    )
    plain_below = hop(up_y1, dz=1)
    plain_above = hop(down_y0, dz=-1)
    away_own = term_blocks(tokens_in, after(first_part, up_y0), own, other)
    came_own = hop(away_own, dc=1)
    pair_cross = term_blocks(
        tokens_in, after(second_part, away_own), cross, core, came_second[:4], stacked=True
    )
    crossed = hop(pair_cross, dy=1)
    pair_straight = term_blocks(
        tokens_in, after(second_part, pair_cross), straight, core, came_second[4:], stacked=True
    )
    own_y0, own_y1 = term_blocks(tokens_in, after(first_part, pair_straight), own, core, came_own)

    below = after(below, early)
    merged_below = hop(add(up_y0, below).astype(bf16), dz=1)
    merged_above = hop(add(down_y1, above).astype(bf16), dz=-1)
    sent = add(own_y1, plain_below, merged_above).astype(bf16)
    first_sum = add(own_y0, merged_below, plain_above, hop(sent, dy=1))

    half = pair_straight.shape[1] // 2
    both = [
        (add(pair_straight[i, :half], crossed[i, :half]), add(pair_straight[i, half:], crossed[i, half:]))
        for i in range(4)
    ]
    two, up, down = [[value.astype(bf16) for value in pair] for pair in both[:3]]
    from_below = hop(two[0], dz=1)
    from_above = hop(two[1], dz=-1)
    plain_below = hop(up[1], dz=1)
    plain_above = hop(down[0], dz=-1)
    merged_below = hop(add(up[0], from_below).astype(bf16), dz=1)
    merged_above = hop(add(down[1], from_above).astype(bf16), dz=-1)
    second_sum = jnp.concatenate(
        [add(both[3][0], merged_below, plain_above), add(both[3][1], plain_below, merged_above)]
    )
    return first_sum, second_sum


def grad_of_inputs(cotangent, weights, across, wide, *earlier):
    me = lax.axis_index("fsdp")
    y, z, core = me // (2 * NZ), (me // 2) % NZ, me % 2
    mine = after(jnp.stack([weights, across]), *earlier)
    below = hop(mine, dz=1)
    above = hop(mine, dz=-1)
    far = (hop(below[:1], dz=1), hop(above[1:], dz=-1))
    grad = None
    for dz, stack in ((0, mine), (3, below), (1, above), (2, far)):
        stacks = stack if dz == 2 else (stack,)
        stacks = stacks + tuple(hop(part, dc=1) for part in stacks)
        places = [place(y + dy, z + dz, core + dc) for dc in range(2) for dy in range(2)]
        grad = grad_blocks(cotangent, stacks, places, wide, grad)
    return grad


def per_device(inputs, grad_keys, local_weights, feedback, base, momentum, warm_start):
    tokens_in = inputs[0]
    cotangent = grad_keys[0]
    weights = local_weights[0]
    rep_size, fsdp_size = lax.axis_size("rep"), lax.axis_size("fsdp")
    everyone = rep_size * fsdp_size
    rows, width = weights.shape
    my_rep = lax.axis_index("rep")
    block_width = base.shape[1]

    across = hop(weights, dy=1)
    drift = feedback[0].astype(f32) - weights.astype(f32)
    based = lax.dynamic_update_slice_in_dim(
        drift,
        lax.dynamic_slice_in_dim(drift, my_rep * block_width, block_width, 1) + rep_size * base,
        my_rep * block_width,
        1,
    )
    early_sum = scatter_sum(based, "rep", rep_size)

    sums = reduce_terms(tokens_in, cotangent, early_sum)
    inner_sum = jnp.concatenate(
        [scatter_sum(part.astype(bf16), "rep", rep_size) for part in sums], axis=1
    )
    pseudo_mean = (early_sum + inner_rate * inner_sum) / rep_size
    inner_grad = jnp.concatenate(sums, axis=1)
    grad_inputs = grad_of_inputs(cotangent, weights, across, tokens_in.shape[1], *sums)[None]
    full_base = lax.all_gather(base, "rep", axis=1, tiled=True)
    pseudo = full_base + drift + inner_rate * inner_grad

    factor = warm_start
    rank = factor.shape[1]
    everything = ("rep", "fsdp")
    for repeat in range(ROUNDS):
        left_part = dot(pseudo_mean, factor)
        raised = dot(pseudo_mean, left_part, ((0,), (0,)))
        gram_part = dot(left_part, left_part, ((0,), (0,)))
        packed = jnp.concatenate(
            [raised, jnp.tile(gram_part, (raised.shape[0] // rank, 1))], axis=1
        )
        summed = gather_rows(scatter_sum(packed, everything, everyone), everything, everyone)
        lower_factor = jnp.linalg.cholesky(summed[:rank, rank:])
        factor = orthonormal_part(summed[:, :rank], lower_factor)
    left = gather_rows(left_part, "rep", rep_size)
    orthonormal = orthonormal_part(left, lower_factor)

    approx = dot(orthonormal, factor, ((1,), (1,)))
    feedback_out = (pseudo - approx)[None]
    column_block = lax.dynamic_slice_in_dim(approx, my_rep * block_width, block_width, 1)
    momentum_out = momentum_keep * momentum + column_block
    base_out = base - outer_rate * (column_block + momentum_keep * momentum_out)
    return (grad_inputs, feedback_out, base_out, momentum_out, factor)


def solution(mesh):
    split = P("rep", "fsdp", None)
    shared = P("fsdp", "rep")
    return jax.shard_map(
        per_device,
        mesh=mesh,
        in_specs=(split, split, split, split, shared, shared, P()),
        out_specs=(split, split, shared, shared, P()),
        check_vma=False,
    )
```

```python
import functools
import math

import jax
import jax.numpy as jnp
from jax import lax
from jax.experimental import pallas as pl
from jax.experimental.pallas import tpu as pltpu
from jax.sharding import PartitionSpec as P

D = 8192
ROUNDS = 2

outer_rate = 0.7
momentum_keep = 0.9
inner_rate = 0.5
inv_root = 1.0 / math.sqrt(D)

f32 = jnp.float32
bf16 = jnp.bfloat16

NZ = 4
FIRST = 384
PLACES = [(y, z, c) for y in range(2) for z in range(NZ) for c in range(2)]


def place(y, z, c):
    return ((y % 2) * NZ + z % NZ) * 2 + c % 2


def hop(value, dy=0, dz=0, dc=0):
    pairs = [(place(y, z, c), place(y + dy, z + dz, c + dc)) for y, z, c in PLACES]
    return lax.ppermute(value, "fsdp", pairs)


def dot(a, b, dims=((1,), (0,))):
    return lax.dot_general(
        a, b, (dims, ((), ())), precision=lax.Precision.HIGHEST, preferred_element_type=f32
    )


def scatter_sum(value, axes, parts):
    got = lax.all_to_all(value, axes, 0, 0, tiled=True)
    return got.reshape(parts, -1, value.shape[1]).astype(f32).sum(0)


def gather_rows(value, axes, parts):
    rows, width = value.shape
    sent = jnp.broadcast_to(value[None], (parts, rows, width)).reshape(parts * rows, width)
    return lax.all_to_all(sent, axes, 0, 0, tiled=True)


def after(value, *others):
    return lax.optimization_barrier((value,) + others)[0]


def all_spots():
    table = [
        [place(y + dy, z + dz, c + dc) for dc in range(2) for dy in range(2) for dz in range(NZ)]
        for y, z, c in PLACES
    ]
    return lax.dynamic_index_in_dim(
        jnp.array(table, jnp.int32), lax.axis_index("fsdp"), 0, keepdims=False
    )


BLOCKS = {
    "up": [(0, 2), (1, 1), (0, 1), (1, 0)],
    "down": [(1, 2), (0, 3), (1, 3), (0, 0)],
}
COUNT = 4


def pick(values, i):
    return sum(value * (i == at).astype(jnp.int32) for at, value in enumerate(values))


def term_of(tokens, cotangent):
    return inv_root * lax.dot_general(
        tokens[...], cotangent[...], (((0,), (0,)), ((), ())), preferred_element_type=f32
    )


def away_kernel(spots, tokens, cotangent, out):
    out[0] = term_of(tokens, cotangent).astype(bf16)


def pair_kernel(crosses, spots, tokens, cotangent, came, sent, kept, last, straight, cross):
    total = (term_of(tokens, cotangent) + came[0].astype(f32)).astype(bf16)
    first, second = total[:FIRST], total[FIRST:]
    step = pl.program_id(0)
    for index in range(COUNT):

        @pl.when(step == index)
        def _():
            if index < 2:
                sent[index] = first
            else:
                (kept, last)[index - 2][...] = first
            (cross if crosses[index] else straight)[sum(c == crosses[index] for c in crosses[:index])] = second


def term_blocks(tokens_in, cotangent, spots, kind, came=None):
    depth, wide = tokens_in.shape
    rows = wide // len(PLACES)
    width = cotangent.shape[1]
    offset = len(PLACES) // 2 if came is None else 0
    blocks = BLOCKS[kind]
    places = [offset + dy * NZ + dz for dy, dz in blocks]
    in_specs = [
        pl.BlockSpec((depth, rows), lambda i, spots: (0, spots[pick(places, i)])),
        pl.BlockSpec((depth, width), lambda i, spots: (0, 0)),
    ]
    operands = [tokens_in, cotangent]
    whole = pl.BlockSpec((1, rows, width), lambda i, spots: (i, 0, 0))
    if came is None:
        kernel = away_kernel
        out_specs = whole
        out_shape = jax.ShapeDtypeStruct((COUNT, rows, width), bf16)
    else:
        kernel = functools.partial(pair_kernel, [dy for dy, _ in blocks])
        in_specs.append(whole)
        operands.append(came)
        rest = rows - FIRST
        shapes = [(2, FIRST, width)] + [(FIRST, width)] * 2 + [(2, rest, width)] * 2
        out_specs = [
            pl.BlockSpec(shape, lambda i, spots, zeros=(0,) * len(shape): zeros) for shape in shapes
        ]
        out_shape = [jax.ShapeDtypeStruct(shape, bf16) for shape in shapes]
    return pl.pallas_call(
        kernel,
        grid_spec=pltpu.PrefetchScalarGridSpec(
            num_scalar_prefetch=1, grid=(COUNT,), in_specs=in_specs, out_specs=out_specs
        ),
        out_shape=out_shape,
        compiler_params=pltpu.CompilerParams(vmem_limit_bytes=56 << 20),
        cost_estimate=pl.CostEstimate(
            flops=2 * COUNT * depth * rows * width,
            bytes_accessed=2 * COUNT * (depth * rows + 2 * rows * width),
            transcendentals=0,
        ),
    )(spots, *operands)


def grad_kernel(cotangent, block, out):
    product = lax.dot_general(
        cotangent[...], block[...], (((1,), (1,)), ((), ())), preferred_element_type=f32
    )
    out[...] = (inv_root * product).astype(bf16)


def grad_of_inputs(cotangent, every_row):
    tokens, depth = cotangent.shape
    wide = every_row.shape[0]
    rows = 1024
    return pl.pallas_call(
        grad_kernel,
        grid=(wide // rows,),
        in_specs=[
            pl.BlockSpec((tokens, depth), lambda i: (0, 0)),
            pl.BlockSpec((rows, depth), lambda i: (i, 0)),
        ],
        out_specs=pl.BlockSpec((tokens, rows), lambda i: (0, i)),
        out_shape=jax.ShapeDtypeStruct((tokens, wide), bf16),
        compiler_params=pltpu.CompilerParams(vmem_limit_bytes=56 << 20),
        cost_estimate=pl.CostEstimate(
            flops=2 * tokens * depth * wide,
            bytes_accessed=2 * wide * (depth + tokens),
            transcendentals=0,
        ),
    )(cotangent, every_row)


def inverse_of_lower_factor(gram):
    rank = gram.shape[0]
    row = lax.broadcasted_iota(jnp.int32, (rank, rank), 0)
    lane = lax.broadcasted_iota(jnp.int32, (rank, rank), 1)
    work = jnp.concatenate([gram, (row == lane).astype(f32)], axis=1)
    tall = lax.broadcasted_iota(jnp.int32, (rank, 1), 0)
    scales = jnp.zeros((rank, 1), f32)
    for step in range(rank):
        column = work[:, step : step + 1]
        pivot = work[step : step + 1, step : step + 1]
        scales = jnp.where(tall == step, lax.rsqrt(pivot), scales)
        ratio = jnp.where(tall > step, column / pivot, 0.0)
        work = work - ratio * work[step : step + 1, :]
    return work[:, rank:] * scales


def round_kernel(last, summed, mean, *outs):
    rank = summed.shape[1] // 2
    inverse = inverse_of_lower_factor(summed[:rank, rank:])
    factor = dot(summed[:, :rank], inverse, ((1,), (1,)))
    if last:
        outs[0][...] = factor
        outs[1][...] = inverse
        return
    product_kernel_body(mean[...], factor, *outs)


def product_kernel_body(mean, factor, packed, left):
    rank = factor.shape[1]
    left_part = dot(mean, factor)
    left[...] = left_part
    gram = dot(left_part, left_part, ((0,), (0,)))
    raised = dot(mean, left_part, ((0,), (0,)))
    packed[:, :rank] = raised
    packed[:, rank:] = jnp.tile(gram, (raised.shape[0] // rank, 1))


def first_kernel(mean, factor, packed, left):
    product_kernel_body(mean[...], factor[...], packed, left)


def small_call(kernel, out_shapes, *operands):
    return pl.pallas_call(
        kernel,
        out_shape=[jax.ShapeDtypeStruct(shape, f32) for shape in out_shapes],
        compiler_params=pltpu.CompilerParams(vmem_limit_bytes=32 << 20),
        cost_estimate=pl.CostEstimate(
            flops=10**9, bytes_accessed=2 << 20, transcendentals=0
        ),
    )(*operands)


def add(*values):
    total = values[0].astype(f32)
    for value in values[1:]:
        total = total + value.astype(f32)
    return total


def reduce_terms(tokens_in, cotangent, spots):
    blocks = functools.partial(term_blocks, tokens_in)
    away_up = blocks(cotangent, spots, "up")
    came_up = hop(away_up, dc=1)
    away_down = blocks(after(cotangent, away_up), spots, "down")
    came_down = hop(after(away_down, came_up), dc=1)
    sent_up, up_y0, own_y1, up_straight, up_cross = blocks(
        after(cotangent, away_down), spots, "up", came_up
    )
    below = hop(sent_up, dz=1)
    up_crossed = hop(up_cross, dy=1)
    sent_down, down_y1, own_y0, down_straight, down_cross = blocks(
        after(cotangent, up_y0), spots, "down", came_down
    )
    above = hop(sent_down, dz=-1)
    down_crossed = hop(down_cross, dy=1)

    below, above, up_crossed, down_crossed = lax.optimization_barrier(
        (below, above, up_crossed, down_crossed)
    )
    half = up_straight.shape[1] // 2

    def both(straight, crossed):
        total = add(straight, crossed)
        return total[:half], total[half:]

    two_up, two_down = both(up_straight[0], down_crossed[0])
    up_up, up_down = both(up_straight[1], up_crossed[0])
    down_up, down_down = both(down_straight[0], down_crossed[1])
    sent_up = jnp.concatenate([add(up_y0, below[0]), two_up, up_down]).astype(bf16)
    sent_down = jnp.concatenate([add(down_y1, above[0]), two_down, down_up]).astype(bf16)
    below_again, above_again = hop(sent_up, dz=1), hop(sent_down, dz=-1)
    own_second = add(down_straight[1], up_crossed[1])

    below_again, above_again, own_second = lax.optimization_barrier(
        (below_again, above_again, own_second)
    )
    sent = add(own_y1, below[1], above_again[:FIRST]).astype(bf16)
    second_up = add(up_up, below_again[FIRST : FIRST + half]).astype(bf16)
    second_down = add(down_down, above_again[FIRST : FIRST + half]).astype(bf16)
    crossed = hop(sent, dy=1)
    last_below, last_above = hop(second_up, dz=1), hop(second_down, dz=-1)

    second_sum = own_second + jnp.concatenate(
        [add(last_below, above_again[FIRST + half :]), add(below_again[FIRST + half :], last_above)]
    )
    first_sum = add(own_y0, below_again[:FIRST], above[1], crossed)
    return first_sum, second_sum, sent


def per_device(inputs, grad_keys, local_weights, feedback, base, momentum, warm_start):
    tokens_in = inputs[0]
    cotangent = grad_keys[0]
    weights = local_weights[0]
    wide = tokens_in.shape[1]
    rep_size, fsdp_size = lax.axis_size("rep"), lax.axis_size("fsdp")
    everyone = rep_size * fsdp_size
    rows, width = weights.shape
    rank = warm_start.shape[1]
    my_rep = lax.axis_index("rep")
    block_width = base.shape[1]
    everything = ("rep", "fsdp")
    spots = all_spots()

    first_sum, second_sum, sent = reduce_terms(tokens_in, cotangent, spots)

    lane = lax.broadcasted_iota(jnp.int32, (1, width), 1)
    mine = lane // block_width == my_rep
    drift = feedback[0].astype(f32) - weights.astype(f32)
    own_base = jnp.where(mine, jnp.tile(rep_size * base, (1, width // block_width)), 0.0)
    moved = drift + inner_rate * jnp.concatenate([first_sum, second_sum])
    mean = scatter_sum(moved + own_base, "rep", rep_size) / rep_size

    def product_shapes():
        return (width, 2 * rank), (rows // rep_size, rank)

    packed, left_part = small_call(first_kernel, product_shapes(), mean, warm_start)
    full_base = lax.all_gather(after(base, mean), "rep", axis=1, tiled=True)
    every_row = lax.all_gather(local_weights, "fsdp", axis=1, tiled=True)[0]
    grad = grad_of_inputs(after(cotangent, packed), every_row)
    for repeat in range(ROUNDS - 1):
        share = scatter_sum(packed, everything, everyone)
        summed = gather_rows(share, everything, everyone)
        summed, grad = lax.optimization_barrier((summed, grad))
        packed, left_part = small_call(
            functools.partial(round_kernel, False), product_shapes(), summed, mean
        )
    share = scatter_sum(packed, everything, everyone)
    summed = gather_rows(share, everything, everyone)
    left = gather_rows(after(left_part, share), "rep", rep_size)
    factor, inverse = small_call(
        functools.partial(round_kernel, True), ((width, rank), (rank, rank)), summed, mean
    )
    orthonormal = dot(left, inverse, ((1,), (1,)))
    approx = dot(orthonormal, factor, ((1,), (1,)))
    feedback_out = (full_base + moved - approx)[None]
    column_block = lax.dynamic_slice_in_dim(approx, my_rep * block_width, block_width, 1)
    momentum_out = momentum_keep * momentum + column_block
    base_out = base - outer_rate * (column_block + momentum_keep * momentum_out)
    return (grad[None], feedback_out, base_out, momentum_out, factor)


def solution(mesh):
    split = P("rep", "fsdp", None)
    shared = P("fsdp", "rep")
    return jax.shard_map(
        per_device,
        mesh=mesh,
        in_specs=(split, split, split, split, shared, shared, P()),
        out_specs=(split, split, shared, shared, P()),
        check_vma=False,
    )
```

```python
import functools
import math

import jax
import jax.numpy as jnp
from jax import lax
from jax.experimental import pallas as pl
from jax.experimental.pallas import tpu as pltpu
from jax.sharding import PartitionSpec as P

D = 8192
ROUNDS = 2

outer_rate = 0.7
momentum_keep = 0.9
inner_rate = 0.5
inv_root = 1.0 / math.sqrt(D)

f32 = jnp.float32
bf16 = jnp.bfloat16

NZ = 4
FIRST = 320
PLACES = [(y, z, c) for y in range(2) for z in range(NZ) for c in range(2)]


def place(y, z, c):
    return ((y % 2) * NZ + z % NZ) * 2 + c % 2


def hop(value, dy=0, dz=0, dc=0):
    pairs = [(place(y, z, c), place(y + dy, z + dz, c + dc)) for y, z, c in PLACES]
    return lax.ppermute(value, "fsdp", pairs)


def dot(a, b, dims=((1,), (0,))):
    return lax.dot_general(
        a, b, (dims, ((), ())), precision=lax.Precision.HIGHEST, preferred_element_type=f32
    )


def scatter_sum(value, axes, parts):
    got = lax.all_to_all(value, axes, 0, 0, tiled=True)
    return got.reshape(parts, -1, value.shape[1]).astype(f32).sum(0)


def gather_rows(value, axes, parts):
    rows, width = value.shape
    sent = jnp.broadcast_to(value[None], (parts, rows, width)).reshape(parts * rows, width)
    return lax.all_to_all(sent, axes, 0, 0, tiled=True)


def after(value, *others):
    return lax.optimization_barrier((value,) + others)[0]


def all_spots():
    table = [
        [place(y + dy, z + dz, c + dc) for dc in range(2) for dy in range(2) for dz in range(NZ)]
        for y, z, c in PLACES
    ]
    return lax.dynamic_index_in_dim(
        jnp.array(table, jnp.int32), lax.axis_index("fsdp"), 0, keepdims=False
    )


BLOCKS = {
    "up": [(0, 2), (1, 1), (0, 1), (1, 0)],
    "down": [(1, 2), (0, 3), (1, 3), (0, 0)],
}
COUNT = 4


def pick(values, i):
    return sum(value * (i == at).astype(jnp.int32) for at, value in enumerate(values))


def term_of(tokens, cotangent):
    return inv_root * lax.dot_general(
        tokens[...], cotangent[...], (((0,), (0,)), ((), ())), preferred_element_type=f32
    )


def away_kernel(spots, tokens, cotangent, out):
    out[0] = term_of(tokens, cotangent).astype(bf16)


def pair_kernel(crosses, spots, tokens, cotangent, came, sent, kept, last, straight, cross):
    total = (term_of(tokens, cotangent) + came[0].astype(f32)).astype(bf16)
    first, second = total[:FIRST], total[FIRST:]
    step = pl.program_id(0)
    for index in range(COUNT):

        @pl.when(step == index)
        def _():
            if index < 2:
                sent[index] = first
            else:
                (kept, last)[index - 2][...] = first
            (cross if crosses[index] else straight)[sum(c == crosses[index] for c in crosses[:index])] = second


def term_blocks(tokens_in, cotangent, spots, kind, came=None):
    depth, wide = tokens_in.shape
    rows = wide // len(PLACES)
    width = cotangent.shape[1]
    offset = len(PLACES) // 2 if came is None else 0
    blocks = BLOCKS[kind]
    places = [offset + dy * NZ + dz for dy, dz in blocks]
    in_specs = [
        pl.BlockSpec((depth, rows), lambda i, spots: (0, spots[pick(places, i)])),
        pl.BlockSpec((depth, width), lambda i, spots: (0, 0)),
    ]
    operands = [tokens_in, cotangent]
    whole = pl.BlockSpec((1, rows, width), lambda i, spots: (i, 0, 0))
    if came is None:
        kernel = away_kernel
        out_specs = whole
        out_shape = jax.ShapeDtypeStruct((COUNT, rows, width), bf16)
    else:
        kernel = functools.partial(pair_kernel, [dy for dy, _ in blocks])
        in_specs.append(whole)
        operands.append(came)
        rest = rows - FIRST
        shapes = [(2, FIRST, width)] + [(FIRST, width)] * 2 + [(2, rest, width)] * 2
        out_specs = [
            pl.BlockSpec(shape, lambda i, spots, zeros=(0,) * len(shape): zeros) for shape in shapes
        ]
        out_shape = [jax.ShapeDtypeStruct(shape, bf16) for shape in shapes]
    return pl.pallas_call(
        kernel,
        grid_spec=pltpu.PrefetchScalarGridSpec(
            num_scalar_prefetch=1, grid=(COUNT,), in_specs=in_specs, out_specs=out_specs
        ),
        out_shape=out_shape,
        compiler_params=pltpu.CompilerParams(vmem_limit_bytes=56 << 20),
        cost_estimate=pl.CostEstimate(
            flops=2 * COUNT * depth * rows * width,
            bytes_accessed=2 * COUNT * (depth * rows + 2 * rows * width),
            transcendentals=0,
        ),
    )(spots, *operands)


def grad_kernel(cotangent, block, *refs):
    product = lax.dot_general(
        cotangent[...], block[...], (((1,), (1,)), ((), ())), preferred_element_type=f32
    )
    refs[-1][...] = (inv_root * product).astype(bf16)


def half_of_grad(cotangent, every_row, which, before=None):
    tokens, depth = cotangent.shape
    wide = every_row.shape[0]
    rows = 1024
    steps = wide // rows // 2
    in_specs = [
        pl.BlockSpec((tokens, depth), lambda i: (0, 0)),
        pl.BlockSpec((rows, depth), lambda i: (i + which * steps, 0)),
    ]
    operands = [cotangent, every_row]
    aliases = {}
    if before is not None:
        in_specs.append(pl.BlockSpec(memory_space=pl.ANY))
        aliases = {len(operands): 0}
        operands.append(before)
    return pl.pallas_call(
        grad_kernel,
        grid=(steps,),
        in_specs=in_specs,
        out_specs=pl.BlockSpec((tokens, rows), lambda i: (0, i + which * steps)),
        out_shape=jax.ShapeDtypeStruct((tokens, wide), bf16),
        input_output_aliases=aliases,
        compiler_params=pltpu.CompilerParams(vmem_limit_bytes=56 << 20),
        cost_estimate=pl.CostEstimate(
            flops=tokens * depth * wide,
            bytes_accessed=wide * (depth + tokens),
            transcendentals=0,
        ),
    )(*operands)


def final_kernel(
    my_rep, left, inverse, factor, moved, full_base, base, momentum, feedback_out, base_out, momentum_out
):
    orthonormal = dot(left[:, : inverse.shape[0]], inverse[...], ((1,), (1,)))
    approx = dot(orthonormal, factor[...], ((1,), (1,)))
    feedback_out[...] = full_base[...] + moved[...] - approx
    width = base.shape[1]
    columns = factor[pl.ds(pl.multiple_of(my_rep[0] * width, width), width), :]
    approx = dot(orthonormal, columns, ((1,), (1,)))
    moment = momentum_keep * momentum[...] + approx
    momentum_out[...] = moment
    base_out[...] = base[...] - outer_rate * (approx + momentum_keep * moment)


def final_outputs(my_rep, left, inverse, factor, moved, full_base, base, momentum):
    rows, width = moved.shape
    step = 128

    def by_rows(array):
        return pl.BlockSpec((step, array.shape[1]), lambda i, my_rep: (i, 0))

    def whole(array):
        return pl.BlockSpec(array.shape, lambda i, my_rep: (0, 0))

    return pl.pallas_call(
        final_kernel,
        grid_spec=pltpu.PrefetchScalarGridSpec(
            num_scalar_prefetch=1,
            grid=(rows // step,),
            in_specs=[
                by_rows(left), whole(inverse), whole(factor), by_rows(moved), by_rows(full_base),
                by_rows(base), by_rows(momentum),
            ],
            out_specs=[by_rows(moved), by_rows(base), by_rows(momentum)],
        ),
        out_shape=[jax.ShapeDtypeStruct(array.shape, f32) for array in (moved, base, momentum)],
        compiler_params=pltpu.CompilerParams(vmem_limit_bytes=32 << 20),
        cost_estimate=pl.CostEstimate(flops=10**9, bytes_accessed=8 << 20, transcendentals=0),
    )(my_rep.reshape(1).astype(jnp.int32), left, inverse, factor, moved, full_base, base, momentum)


def inverse_of_lower_factor(gram):
    rank = gram.shape[0]
    row = lax.broadcasted_iota(jnp.int32, (rank, rank), 0)
    lane = lax.broadcasted_iota(jnp.int32, (rank, rank), 1)
    work = jnp.concatenate([gram, (row == lane).astype(f32)], axis=1)
    tall = lax.broadcasted_iota(jnp.int32, (rank, 1), 0)
    scales = jnp.zeros((rank, 1), f32)
    for step in range(rank):
        column = work[:, step : step + 1]
        pivot = work[step : step + 1, step : step + 1]
        scales = jnp.where(tall == step, lax.rsqrt(pivot), scales)
        ratio = jnp.where(tall > step, column / pivot, 0.0)
        work = work - ratio * work[step : step + 1, :]
    return work[:, rank:] * scales


def round_kernel(last, summed, mean, *outs):
    rank = summed.shape[1] // 2
    inverse = inverse_of_lower_factor(summed[:rank, rank:])
    factor = dot(summed[:, :rank], inverse, ((1,), (1,)))
    if last:
        outs[0][...] = factor
        outs[1][...] = inverse
        return
    product_kernel_body(mean[...], factor, *outs)


def product_kernel_body(mean, factor, packed, left):
    rank = factor.shape[1]
    left_part = dot(mean, factor)
    left[...] = jnp.concatenate([left_part, left_part], axis=1)
    gram = dot(left_part, left_part, ((0,), (0,)))
    raised = dot(mean, left_part, ((0,), (0,)))
    packed[:, :rank] = raised
    packed[:, rank:] = jnp.tile(gram, (raised.shape[0] // rank, 1))


def first_kernel(mean, factor, packed, left):
    product_kernel_body(mean[...], factor[...], packed, left)


def small_call(kernel, out_shapes, *operands):
    return pl.pallas_call(
        kernel,
        out_shape=[jax.ShapeDtypeStruct(shape, f32) for shape in out_shapes],
        compiler_params=pltpu.CompilerParams(vmem_limit_bytes=32 << 20),
        cost_estimate=pl.CostEstimate(
            flops=10**9, bytes_accessed=2 << 20, transcendentals=0
        ),
    )(*operands)


def add(*values):
    total = values[0].astype(f32)
    for value in values[1:]:
        total = total + value.astype(f32)
    return total


def reduce_terms(tokens_in, cotangent, spots, early_of):
    blocks = functools.partial(term_blocks, tokens_in)
    away_up = blocks(cotangent, spots, "up")
    came_up = hop(away_up, dc=1)
    away_down = blocks(after(cotangent, away_up), spots, "down")
    came_down = hop(after(away_down, came_up), dc=1)
    sent_up, up_y0, own_y1, up_straight, up_cross = blocks(
        after(cotangent, away_down), spots, "up", came_up
    )
    below = hop(sent_up, dz=1)
    up_crossed = hop(up_cross, dy=1)
    sent_down, down_y1, own_y0, down_straight, down_cross = blocks(
        after(cotangent, up_y0), spots, "down", came_down
    )
    above = hop(sent_down, dz=-1)
    down_crossed = hop(down_cross, dy=1)

    below, above, up_crossed, down_crossed = lax.optimization_barrier(
        (below, above, up_crossed, down_crossed)
    )
    half = up_straight.shape[1] // 2

    def both(straight, crossed):
        total = add(straight, crossed)
        return total[:half], total[half:]

    two_up, two_down = both(up_straight[0], down_crossed[0])
    up_up, up_down = both(up_straight[1], up_crossed[0])
    down_up, down_down = both(down_straight[0], down_crossed[1])
    sent_up = jnp.concatenate([add(up_y0, below[0]), two_up, up_down]).astype(bf16)
    sent_down = jnp.concatenate([add(down_y1, above[0]), two_down, down_up]).astype(bf16)
    below_again, above_again = hop(sent_up, dz=1), hop(sent_down, dz=-1)
    own_second = add(down_straight[1], up_crossed[1])

    early, below_again, above_again, own_second = lax.optimization_barrier(
        (early_of(sent_up, sent_down), below_again, above_again, own_second)
    )
    sent = add(own_y1, below[1], above_again[:FIRST]).astype(bf16)
    second_up = add(up_up, below_again[FIRST : FIRST + half]).astype(bf16)
    second_down = add(down_down, above_again[FIRST : FIRST + half]).astype(bf16)
    crossed = hop(sent, dy=1)
    last_below, last_above = hop(second_up, dz=1), hop(second_down, dz=-1)

    second_sum = own_second + jnp.concatenate(
        [add(last_below, above_again[FIRST + half :]), add(below_again[FIRST + half :], last_above)]
    )
    first_sum = add(own_y0, below_again[:FIRST], above[1], crossed)
    return first_sum, second_sum, early


def per_device(inputs, grad_keys, local_weights, feedback, base, momentum, warm_start):
    tokens_in = inputs[0]
    cotangent = grad_keys[0]
    weights = local_weights[0]
    wide = tokens_in.shape[1]
    rep_size, fsdp_size = lax.axis_size("rep"), lax.axis_size("fsdp")
    everyone = rep_size * fsdp_size
    rows, width = weights.shape
    rank = warm_start.shape[1]
    my_rep = lax.axis_index("rep")
    block_width = base.shape[1]
    everything = ("rep", "fsdp")
    spots = all_spots()

    lane = lax.broadcasted_iota(jnp.int32, (1, width), 1)
    mine = lane // block_width == my_rep
    drift = feedback[0].astype(f32) - weights.astype(f32)

    def early_of(*behind):
        own_base = jnp.where(mine, jnp.tile(rep_size * base, (1, width // block_width)), 0.0)
        return scatter_sum(after(drift + own_base, *behind), "rep", rep_size)

    first_sum, second_sum, early = reduce_terms(tokens_in, cotangent, spots, early_of)
    inner_grad = jnp.concatenate([first_sum, second_sum])
    mean = (
        early + inner_rate * scatter_sum(inner_grad.astype(bf16), "rep", rep_size)
    ) / rep_size
    moved = drift + inner_rate * inner_grad

    def product_shapes():
        return (width, 2 * rank), (rows // rep_size, 2 * rank)

    packed, left_part = small_call(first_kernel, product_shapes(), mean, warm_start)
    full_base = lax.all_gather(after(base, mean), "rep", axis=1, tiled=True)
    every_row = lax.all_gather(local_weights, "fsdp", axis=1, tiled=True)[0]
    grad = None
    for repeat in range(ROUNDS):
        if repeat < 2:
            grad = half_of_grad(after(cotangent, packed), every_row, repeat, grad)
        summed = gather_rows(scatter_sum(packed, everything, everyone), everything, everyone)
        summed, grad = lax.optimization_barrier((summed, grad))
        if repeat < ROUNDS - 1:
            packed, left_part = small_call(
                functools.partial(round_kernel, False), product_shapes(), summed, mean
            )
    left = gather_rows(after(left_part, summed), "rep", rep_size)
    factor, inverse = small_call(
        functools.partial(round_kernel, True), ((width, rank), (rank, rank)), summed, mean
    )
    feedback_out, base_out, momentum_out = final_outputs(
        my_rep, left, inverse, factor, moved, full_base, base, momentum
    )
    return (grad[None], feedback_out[None], base_out, momentum_out, factor)


def solution(mesh):
    split = P("rep", "fsdp", None)
    shared = P("fsdp", "rep")
    return jax.shard_map(
        per_device,
        mesh=mesh,
        in_specs=(split, split, split, split, shared, shared, P()),
        out_specs=(split, split, shared, shared, P()),
        check_vma=False,
    )
```

```python
import functools
import math

import jax
import jax.numpy as jnp
from jax import lax
from jax.experimental import pallas as pl
from jax.experimental.pallas import tpu as pltpu
from jax.sharding import PartitionSpec as P

D = 8192
ROUNDS = 2

outer_rate = 0.7
momentum_keep = 0.9
inner_rate = 0.5
inv_root = 1.0 / math.sqrt(D)

f32 = jnp.float32
bf16 = jnp.bfloat16

NZ = 4
FIRST = 320
PLACES = [(y, z, c) for y in range(2) for z in range(NZ) for c in range(2)]


def place(y, z, c):
    return ((y % 2) * NZ + z % NZ) * 2 + c % 2


def hop(value, dy=0, dz=0, dc=0):
    pairs = [(place(y, z, c), place(y + dy, z + dz, c + dc)) for y, z, c in PLACES]
    return lax.ppermute(value, "fsdp", pairs)


def dot(a, b, dims=((1,), (0,))):
    return lax.dot_general(
        a, b, (dims, ((), ())), precision=lax.Precision.HIGHEST, preferred_element_type=f32
    )


def scatter_sum(value, axes, parts):
    got = lax.all_to_all(value, axes, 0, 0, tiled=True)
    return got.reshape(parts, -1, value.shape[1]).astype(f32).sum(0)


def gather_rows(value, axes, parts):
    rows, width = value.shape
    sent = jnp.broadcast_to(value[None], (parts, rows, width)).reshape(parts * rows, width)
    return lax.all_to_all(sent, axes, 0, 0, tiled=True)


def after(value, *others):
    return lax.optimization_barrier((value,) + others)[0]


def all_spots():
    table = [
        [place(y + dy, z + dz, c + dc) for dc in range(2) for dy in range(2) for dz in range(NZ)]
        for y, z, c in PLACES
    ]
    return lax.dynamic_index_in_dim(
        jnp.array(table, jnp.int32), lax.axis_index("fsdp"), 0, keepdims=False
    )


BLOCKS = {
    "up": [(0, 2), (1, 1), (0, 1), (1, 0)],
    "down": [(1, 2), (0, 3), (1, 3), (0, 0)],
}
COUNT = 4


def pick(values, i):
    return sum(value * (i == at).astype(jnp.int32) for at, value in enumerate(values))


def term_of(tokens, cotangent):
    return inv_root * lax.dot_general(
        tokens[...], cotangent[...], (((0,), (0,)), ((), ())), preferred_element_type=f32
    )


def away_kernel(spots, tokens, cotangent, out):
    out[0] = term_of(tokens, cotangent).astype(bf16)


def pair_kernel(crosses, spots, tokens, cotangent, came, sent, kept, last, straight, cross):
    total = (term_of(tokens, cotangent) + came[0].astype(f32)).astype(bf16)
    first, second = total[:FIRST], total[FIRST:]
    step = pl.program_id(0)
    for index in range(COUNT):

        @pl.when(step == index)
        def _():
            if index < 2:
                sent[index] = first
            else:
                (kept, last)[index - 2][...] = first
            (cross if crosses[index] else straight)[sum(c == crosses[index] for c in crosses[:index])] = second


def term_blocks(tokens_in, cotangent, spots, kind, came=None):
    depth, wide = tokens_in.shape
    rows = wide // len(PLACES)
    width = cotangent.shape[1]
    offset = len(PLACES) // 2 if came is None else 0
    blocks = BLOCKS[kind]
    places = [offset + dy * NZ + dz for dy, dz in blocks]
    in_specs = [
        pl.BlockSpec((depth, rows), lambda i, spots: (0, spots[pick(places, i)])),
        pl.BlockSpec((depth, width), lambda i, spots: (0, 0)),
    ]
    operands = [tokens_in, cotangent]
    whole = pl.BlockSpec((1, rows, width), lambda i, spots: (i, 0, 0))
    if came is None:
        kernel = away_kernel
        out_specs = whole
        out_shape = jax.ShapeDtypeStruct((COUNT, rows, width), bf16)
    else:
        kernel = functools.partial(pair_kernel, [dy for dy, _ in blocks])
        in_specs.append(whole)
        operands.append(came)
        rest = rows - FIRST
        shapes = [(2, FIRST, width)] + [(FIRST, width)] * 2 + [(2, rest, width)] * 2
        out_specs = [
            pl.BlockSpec(shape, lambda i, spots, zeros=(0,) * len(shape): zeros) for shape in shapes
        ]
        out_shape = [jax.ShapeDtypeStruct(shape, bf16) for shape in shapes]
    return pl.pallas_call(
        kernel,
        grid_spec=pltpu.PrefetchScalarGridSpec(
            num_scalar_prefetch=1, grid=(COUNT,), in_specs=in_specs, out_specs=out_specs
        ),
        out_shape=out_shape,
        compiler_params=pltpu.CompilerParams(vmem_limit_bytes=60 << 20),
        cost_estimate=pl.CostEstimate(
            flops=2 * COUNT * depth * rows * width,
            bytes_accessed=2 * COUNT * (depth * rows + 2 * rows * width),
            transcendentals=0,
        ),
    )(spots, *operands)


def grad_kernel(cotangent, block, *refs):
    product = lax.dot_general(
        cotangent[...], block[...], (((1,), (1,)), ((), ())), preferred_element_type=f32
    )
    refs[-1][...] = (inv_root * product).astype(bf16)


def half_of_grad(cotangent, every_row, which, before=None):
    tokens, depth = cotangent.shape
    wide = every_row.shape[0]
    rows = 1024
    steps = wide // rows // 2
    in_specs = [
        pl.BlockSpec((tokens, depth), lambda i: (0, 0)),
        pl.BlockSpec((rows, depth), lambda i: (i + which * steps, 0)),
    ]
    operands = [cotangent, every_row]
    aliases = {}
    if before is not None:
        in_specs.append(pl.BlockSpec(memory_space=pl.ANY))
        aliases = {len(operands): 0}
        operands.append(before)
    return pl.pallas_call(
        grad_kernel,
        grid=(steps,),
        in_specs=in_specs,
        out_specs=pl.BlockSpec((tokens, rows), lambda i: (0, i + which * steps)),
        out_shape=jax.ShapeDtypeStruct((tokens, wide), bf16),
        input_output_aliases=aliases,
        compiler_params=pltpu.CompilerParams(vmem_limit_bytes=60 << 20),
        cost_estimate=pl.CostEstimate(
            flops=tokens * depth * wide,
            bytes_accessed=wide * (depth + tokens),
            transcendentals=0,
        ),
    )(*operands)


def final_kernel(
    my_rep, left, inverse, factor, moved, full_base, base, momentum, feedback_out, base_out, momentum_out
):
    orthonormal = dot(left[:, : inverse.shape[0]], inverse[...], ((1,), (1,)))
    approx = dot(orthonormal, factor[...], ((1,), (1,)))
    feedback_out[...] = full_base[...] + moved[...] - approx
    width = base.shape[1]
    columns = factor[pl.ds(pl.multiple_of(my_rep[0] * width, width), width), :]
    approx = dot(orthonormal, columns, ((1,), (1,)))
    moment = momentum_keep * momentum[...] + approx
    momentum_out[...] = moment
    base_out[...] = base[...] - outer_rate * (approx + momentum_keep * moment)


def final_outputs(my_rep, left, inverse, factor, moved, full_base, base, momentum):
    rows, width = moved.shape
    step = 128

    def by_rows(array):
        return pl.BlockSpec((step, array.shape[1]), lambda i, my_rep: (i, 0))

    def whole(array):
        return pl.BlockSpec(array.shape, lambda i, my_rep: (0, 0))

    return pl.pallas_call(
        final_kernel,
        grid_spec=pltpu.PrefetchScalarGridSpec(
            num_scalar_prefetch=1,
            grid=(rows // step,),
            in_specs=[
                by_rows(left), whole(inverse), whole(factor), by_rows(moved), by_rows(full_base),
                by_rows(base), by_rows(momentum),
            ],
            out_specs=[by_rows(moved), by_rows(base), by_rows(momentum)],
        ),
        out_shape=[jax.ShapeDtypeStruct(array.shape, f32) for array in (moved, base, momentum)],
        compiler_params=pltpu.CompilerParams(vmem_limit_bytes=32 << 20),
        cost_estimate=pl.CostEstimate(flops=10**9, bytes_accessed=8 << 20, transcendentals=0),
    )(my_rep.reshape(1).astype(jnp.int32), left, inverse, factor, moved, full_base, base, momentum)


def inverse_of_lower_factor(gram):
    rank = gram.shape[0]
    row = lax.broadcasted_iota(jnp.int32, (rank, rank), 0)
    lane = lax.broadcasted_iota(jnp.int32, (rank, rank), 1)
    work = jnp.concatenate([gram, (row == lane).astype(f32)], axis=1)
    tall = lax.broadcasted_iota(jnp.int32, (rank, 1), 0)
    scales = jnp.zeros((rank, 1), f32)
    for step in range(rank):
        column = work[:, step : step + 1]
        pivot = work[step : step + 1, step : step + 1]
        scales = jnp.where(tall == step, lax.rsqrt(pivot), scales)
        ratio = jnp.where(tall > step, column / pivot, 0.0)
        work = work - ratio * work[step : step + 1, :]
    return work[:, rank:] * scales


def round_kernel(last, summed, mean, *outs):
    rank = summed.shape[1] // 2
    inverse = inverse_of_lower_factor(summed[:rank, rank:])
    factor = dot(summed[:, :rank], inverse, ((1,), (1,)))
    if last:
        outs[0][...] = factor
        outs[1][...] = inverse
        return
    product_kernel_body(mean[...], factor, *outs)


def product_kernel_body(mean, factor, packed, left):
    rank = factor.shape[1]
    left_part = dot(mean, factor)
    left[...] = jnp.concatenate([left_part, left_part], axis=1)
    gram = dot(left_part, left_part, ((0,), (0,)))
    raised = dot(mean, left_part, ((0,), (0,)))
    packed[:, :rank] = raised
    packed[:, rank:] = jnp.tile(gram, (raised.shape[0] // rank, 1))


def first_kernel(mean, factor, packed, left):
    product_kernel_body(mean[...], factor[...], packed, left)


def small_call(kernel, out_shapes, *operands):
    return pl.pallas_call(
        kernel,
        out_shape=[jax.ShapeDtypeStruct(shape, f32) for shape in out_shapes],
        compiler_params=pltpu.CompilerParams(vmem_limit_bytes=32 << 20),
        cost_estimate=pl.CostEstimate(
            flops=10**9, bytes_accessed=2 << 20, transcendentals=0
        ),
    )(*operands)


def add(*values):
    total = values[0].astype(f32)
    for value in values[1:]:
        total = total + value.astype(f32)
    return total


def first_stage_kernel(
    up_y0, down_y1, below, above, up_straight, down_straight, up_crossed, down_crossed,
    sent_up, sent_down, up_up, down_down, own,
):
    first = up_y0.shape[0]
    half = up_straight.shape[1] // 2
    sent_up[:first] = add(up_y0[...], below[0]).astype(bf16)
    sent_down[:first] = add(down_y1[...], above[0]).astype(bf16)
    two = add(up_straight[0], down_crossed[0]).astype(bf16)
    up = add(up_straight[1], up_crossed[0])
    down = add(down_straight[0], down_crossed[1])
    sent_up[first : first + half] = two[:half]
    sent_down[first : first + half] = two[half:]
    sent_up[first + half :] = up[half:].astype(bf16)
    sent_down[first + half :] = down[:half].astype(bf16)
    up_up[...] = up[:half]
    down_down[...] = down[half:]
    own[...] = add(down_straight[1], up_crossed[1])


def second_stage_kernel(
    own_y1, plain_below, above_again, below_again, up_up, down_down, sent, second_up, second_down
):
    first = own_y1.shape[0]
    half = up_up.shape[0]
    sent[...] = add(own_y1[...], plain_below[0], above_again[:first]).astype(bf16)
    second_up[...] = add(up_up[...], below_again[first : first + half]).astype(bf16)
    second_down[...] = add(down_down[...], above_again[first : first + half]).astype(bf16)


def stage(kernel, shapes, planes, *operands):
    width = operands[0].shape[-1]
    columns = 256

    def by_columns(shape, plane=None):
        lead = (0,) * (len(shape) - 1)
        if plane is not None:
            shape, lead = (1,) + shape[1:], (plane,) + lead[1:]
        return pl.BlockSpec(shape[:-1] + (columns,), lambda i: lead + (i,))

    return pl.pallas_call(
        kernel,
        grid=(width // columns,),
        in_specs=[by_columns(x.shape, planes.get(at)) for at, x in enumerate(operands)],
        out_specs=[by_columns(shape) for shape, _ in shapes],
        out_shape=[jax.ShapeDtypeStruct(*shape) for shape in shapes],
        compiler_params=pltpu.CompilerParams(vmem_limit_bytes=60 << 20),
        cost_estimate=pl.CostEstimate(flops=10**7, bytes_accessed=8 << 20, transcendentals=0),
    )(*operands)


def reduce_terms(tokens_in, cotangent, spots, early_of):
    blocks = functools.partial(term_blocks, tokens_in)
    away_up = blocks(cotangent, spots, "up")
    came_up = hop(away_up, dc=1)
    away_down = blocks(after(cotangent, away_up), spots, "down")
    came_down = hop(after(away_down, came_up), dc=1)
    sent_up, up_y0, own_y1, up_straight, up_cross = blocks(
        after(cotangent, away_down), spots, "up", came_up
    )
    below = hop(sent_up, dz=1)
    up_crossed = hop(up_cross, dy=1)
    sent_down, down_y1, own_y0, down_straight, down_cross = blocks(
        after(cotangent, up_y0), spots, "down", came_down
    )
    above = hop(sent_down, dz=-1)
    down_crossed = hop(down_cross, dy=1)

    below, above, up_crossed, down_crossed = lax.optimization_barrier(
        (below, above, up_crossed, down_crossed)
    )
    half = up_straight.shape[1] // 2
    rest, width = up_straight.shape[1:]
    sent_up, sent_down, up_up, down_down, own_second = stage(
        first_stage_kernel,
        [((FIRST + rest, width), bf16)] * 2 + [((half, width), f32)] * 2 + [((rest, width), f32)],
        {2: 0, 3: 0},
        up_y0, down_y1, below, above, up_straight, down_straight, up_crossed, down_crossed,
    )
    below_again, above_again = hop(sent_up, dz=1), hop(sent_down, dz=-1)

    early = early_of(sent_up, sent_down)
    below_again, above_again, own_second = lax.optimization_barrier(
        (below_again, above_again, own_second)
    )
    sent, second_up, second_down = stage(
        second_stage_kernel,
        [((FIRST, width), bf16)] + [((half, width), bf16)] * 2,
        {1: 1},
        own_y1, below, above_again, below_again, up_up, down_down,
    )
    crossed = hop(sent, dy=1)
    early, crossed, last_below, last_above = lax.optimization_barrier(
        (early, crossed, hop(second_up, dz=1), hop(second_down, dz=-1))
    )

    second_sum = own_second + jnp.concatenate(
        [add(last_below, above_again[FIRST + half :]), add(below_again[FIRST + half :], last_above)]
    )
    first_sum = add(own_y0, below_again[:FIRST], above[1], crossed)
    return first_sum, second_sum, early


def per_device(inputs, grad_keys, local_weights, feedback, base, momentum, warm_start):
    tokens_in = inputs[0]
    cotangent = grad_keys[0]
    weights = local_weights[0]
    wide = tokens_in.shape[1]
    rep_size, fsdp_size = lax.axis_size("rep"), lax.axis_size("fsdp")
    everyone = rep_size * fsdp_size
    rows, width = weights.shape
    rank = warm_start.shape[1]
    my_rep = lax.axis_index("rep")
    block_width = base.shape[1]
    everything = ("rep", "fsdp")
    spots = all_spots()

    lane = lax.broadcasted_iota(jnp.int32, (1, width), 1)
    mine = lane // block_width == my_rep

    def early_of(*behind):
        drift = feedback[0].astype(f32) - after(weights, *behind).astype(f32)
        own_base = jnp.where(mine, jnp.tile(rep_size * base, (1, width // block_width)), 0.0)
        return scatter_sum(drift + own_base, "rep", rep_size), drift

    first_sum, second_sum, (early, drift) = reduce_terms(tokens_in, cotangent, spots, early_of)
    inner_grad = jnp.concatenate([first_sum, second_sum])
    mean = (
        early + inner_rate * scatter_sum(inner_grad.astype(bf16), "rep", rep_size)
    ) / rep_size
    moved = after(drift, mean) + inner_rate * inner_grad

    def product_shapes():
        return (width, 2 * rank), (rows // rep_size, 2 * rank)

    packed, left_part = small_call(first_kernel, product_shapes(), mean, warm_start)
    full_base = lax.all_gather(after(base, mean), "rep", axis=1, tiled=True)
    every_row = lax.all_gather(local_weights, "fsdp", axis=1, tiled=True)[0]
    grad = None
    for repeat in range(ROUNDS):
        if repeat < 2:
            grad = half_of_grad(after(cotangent, packed), every_row, repeat, grad)
        summed = gather_rows(scatter_sum(packed, everything, everyone), everything, everyone)
        summed, grad, moved = lax.optimization_barrier((summed, grad, moved))
        if repeat < ROUNDS - 1:
            packed, left_part = small_call(
                functools.partial(round_kernel, False), product_shapes(), summed, mean
            )
    left = gather_rows(after(left_part, summed), "rep", rep_size)
    factor, inverse = small_call(
        functools.partial(round_kernel, True), ((width, rank), (rank, rank)), summed, mean
    )
    feedback_out, base_out, momentum_out = final_outputs(
        my_rep, left, inverse, factor, moved, full_base, base, momentum
    )
    return (grad[None], feedback_out[None], base_out, momentum_out, factor)


def solution(mesh):
    split = P("rep", "fsdp", None)
    shared = P("fsdp", "rep")
    return jax.shard_map(
        per_device,
        mesh=mesh,
        in_specs=(split, split, split, split, shared, shared, P()),
        out_specs=(split, split, shared, shared, P()),
        check_vma=False,
    )
```

```python
import functools
import math

import jax
import jax.numpy as jnp
from jax import lax
from jax.experimental import pallas as pl
from jax.experimental.pallas import tpu as pltpu
from jax.sharding import PartitionSpec as P

D = 8192
ROUNDS = 2

outer_rate = 0.7
momentum_keep = 0.9
inner_rate = 0.5
inv_root = 1.0 / math.sqrt(D)

f32 = jnp.float32
bf16 = jnp.bfloat16

NZ = 4
FIRST = 352
PLACES = [(y, z, c) for y in range(2) for z in range(NZ) for c in range(2)]


def place(y, z, c):
    return ((y % 2) * NZ + z % NZ) * 2 + c % 2


def hop(value, dy=0, dz=0, dc=0):
    pairs = [(place(y, z, c), place(y + dy, z + dz, c + dc)) for y, z, c in PLACES]
    return lax.ppermute(value, "fsdp", pairs)


def dot(a, b, dims=((1,), (0,))):
    return lax.dot_general(
        a, b, (dims, ((), ())), precision=lax.Precision.HIGHEST, preferred_element_type=f32
    )


def scatter_sum(value, axes, parts):
    got = lax.all_to_all(value, axes, 0, 0, tiled=True)
    return got.reshape(parts, -1, value.shape[1]).astype(f32).sum(0)


def gather_rows(value, axes, parts):
    rows, width = value.shape
    sent = jnp.broadcast_to(value[None], (parts, rows, width)).reshape(parts * rows, width)
    return lax.all_to_all(sent, axes, 0, 0, tiled=True)


def after(value, *others):
    return lax.optimization_barrier((value,) + others)[0]


def all_spots():
    table = [
        [place(y + dy, z + dz, c + dc) for dc in range(2) for dy in range(2) for dz in range(NZ)]
        for y, z, c in PLACES
    ]
    return lax.dynamic_index_in_dim(
        jnp.array(table, jnp.int32), lax.axis_index("fsdp"), 0, keepdims=False
    )


BLOCKS = {
    "up": [(0, 2), (1, 1), (0, 1), (1, 0)],
    "down": [(1, 2), (0, 3), (1, 3), (0, 0)],
}
COUNT = 4


def pick(values, i):
    return sum(value * (i == at).astype(jnp.int32) for at, value in enumerate(values))


def term_of(tokens, cotangent):
    return inv_root * lax.dot_general(
        tokens[...], cotangent[...], (((0,), (0,)), ((), ())), preferred_element_type=f32
    )


def away_kernel(spots, tokens, cotangent, out):
    out[0] = term_of(tokens, cotangent).astype(bf16)


def pair_kernel(crosses, spots, tokens, cotangent, came, sent, kept, last, straight, cross):
    total = (term_of(tokens, cotangent) + came[0].astype(f32)).astype(bf16)
    first, second = total[:FIRST], total[FIRST:]
    step = pl.program_id(0)
    for index in range(COUNT):

        @pl.when(step == index)
        def _():
            if index < 2:
                sent[index] = first
            else:
                (kept, last)[index - 2][...] = first
            (cross if crosses[index] else straight)[sum(c == crosses[index] for c in crosses[:index])] = second


def term_blocks(tokens_in, cotangent, spots, kind, came=None):
    depth, wide = tokens_in.shape
    rows = wide // len(PLACES)
    width = cotangent.shape[1]
    offset = len(PLACES) // 2 if came is None else 0
    blocks = BLOCKS[kind]
    places = [offset + dy * NZ + dz for dy, dz in blocks]
    in_specs = [
        pl.BlockSpec((depth, rows), lambda i, spots: (0, spots[pick(places, i)])),
        pl.BlockSpec((depth, width), lambda i, spots: (0, 0)),
    ]
    operands = [tokens_in, cotangent]
    whole = pl.BlockSpec((1, rows, width), lambda i, spots: (i, 0, 0))
    if came is None:
        kernel = away_kernel
        out_specs = whole
        out_shape = jax.ShapeDtypeStruct((COUNT, rows, width), bf16)
    else:
        kernel = functools.partial(pair_kernel, [dy for dy, _ in blocks])
        in_specs.append(whole)
        operands.append(came)
        rest = rows - FIRST
        shapes = [(2, FIRST, width)] + [(FIRST, width)] * 2 + [(2, rest, width)] * 2
        out_specs = [
            pl.BlockSpec(shape, lambda i, spots, zeros=(0,) * len(shape): zeros) for shape in shapes
        ]
        out_shape = [jax.ShapeDtypeStruct(shape, bf16) for shape in shapes]
    return pl.pallas_call(
        kernel,
        grid_spec=pltpu.PrefetchScalarGridSpec(
            num_scalar_prefetch=1, grid=(COUNT,), in_specs=in_specs, out_specs=out_specs
        ),
        out_shape=out_shape,
        compiler_params=pltpu.CompilerParams(vmem_limit_bytes=60 << 20),
        cost_estimate=pl.CostEstimate(
            flops=2 * COUNT * depth * rows * width,
            bytes_accessed=2 * COUNT * (depth * rows + 2 * rows * width),
            transcendentals=0,
        ),
    )(spots, *operands)


def grad_kernel(cotangent, block, *refs):
    product = lax.dot_general(
        cotangent[...], block[...], (((1,), (1,)), ((), ())), preferred_element_type=f32
    )
    refs[-1][...] = (inv_root * product).astype(bf16)


def half_of_grad(cotangent, every_row, which, before=None):
    tokens, depth = cotangent.shape
    wide = every_row.shape[0]
    rows = 1024
    steps = wide // rows // 2
    in_specs = [
        pl.BlockSpec((tokens, depth), lambda i: (0, 0)),
        pl.BlockSpec((rows, depth), lambda i: (i + which * steps, 0)),
    ]
    operands = [cotangent, every_row]
    aliases = {}
    if before is not None:
        in_specs.append(pl.BlockSpec(memory_space=pl.ANY))
        aliases = {len(operands): 0}
        operands.append(before)
    return pl.pallas_call(
        grad_kernel,
        grid=(steps,),
        in_specs=in_specs,
        out_specs=pl.BlockSpec((tokens, rows), lambda i: (0, i + which * steps)),
        out_shape=jax.ShapeDtypeStruct((tokens, wide), bf16),
        input_output_aliases=aliases,
        compiler_params=pltpu.CompilerParams(vmem_limit_bytes=60 << 20),
        cost_estimate=pl.CostEstimate(
            flops=tokens * depth * wide,
            bytes_accessed=wide * (depth + tokens),
            transcendentals=0,
        ),
    )(*operands)


def final_kernel(
    my_rep, left, inverse, factor, moved, full_base, base, momentum, feedback_out, base_out, momentum_out
):
    orthonormal = dot(left[:, : inverse.shape[0]], inverse[...], ((1,), (1,)))
    approx = dot(orthonormal, factor[...], ((1,), (1,)))
    feedback_out[...] = full_base[...] + moved[...] - approx
    width = base.shape[1]
    columns = factor[pl.ds(pl.multiple_of(my_rep[0] * width, width), width), :]
    approx = dot(orthonormal, columns, ((1,), (1,)))
    moment = momentum_keep * momentum[...] + approx
    momentum_out[...] = moment
    base_out[...] = base[...] - outer_rate * (approx + momentum_keep * moment)


def final_outputs(my_rep, left, inverse, factor, moved, full_base, base, momentum):
    rows, width = moved.shape
    step = 128

    def by_rows(array):
        return pl.BlockSpec((step, array.shape[1]), lambda i, my_rep: (i, 0))

    def whole(array):
        return pl.BlockSpec(array.shape, lambda i, my_rep: (0, 0))

    return pl.pallas_call(
        final_kernel,
        grid_spec=pltpu.PrefetchScalarGridSpec(
            num_scalar_prefetch=1,
            grid=(rows // step,),
            in_specs=[
                by_rows(left), whole(inverse), whole(factor), by_rows(moved), by_rows(full_base),
                by_rows(base), by_rows(momentum),
            ],
            out_specs=[by_rows(moved), by_rows(base), by_rows(momentum)],
        ),
        out_shape=[jax.ShapeDtypeStruct(array.shape, f32) for array in (moved, base, momentum)],
        compiler_params=pltpu.CompilerParams(vmem_limit_bytes=32 << 20),
        cost_estimate=pl.CostEstimate(flops=10**9, bytes_accessed=8 << 20, transcendentals=0),
    )(my_rep.reshape(1).astype(jnp.int32), left, inverse, factor, moved, full_base, base, momentum)


def inverse_of_lower_factor(gram):
    rank = gram.shape[0]
    row = lax.broadcasted_iota(jnp.int32, (rank, rank), 0)
    lane = lax.broadcasted_iota(jnp.int32, (rank, rank), 1)
    work = jnp.concatenate([gram, (row == lane).astype(f32)], axis=1)
    groups = [work[at : at + 8] for at in range(0, rank, 8)]
    tall = lax.broadcasted_iota(jnp.int32, (8, 1), 0)
    for step in range(rank):
        at, inner = step // 8, step % 8
        pivot_row = groups[at][inner : inner + 1]
        scaled = pivot_row / pivot_row[:, step : step + 1]
        for index in range(at, len(groups)):
            column = groups[index][:, step : step + 1]
            if index == at:
                column = jnp.where(tall > inner, column, 0.0)
            groups[index] = groups[index] - column * scaled
    work = jnp.concatenate(groups)
    pivots = jnp.sum(jnp.where(row == lane, work[:, :rank], 0.0), axis=1, keepdims=True)
    return work[:, rank:] * lax.rsqrt(pivots)


def round_kernel(last, summed, *refs):
    rank = summed.shape[1] // 2
    inverse = inverse_of_lower_factor(summed[:rank, rank:])
    factor = dot(summed[:, :rank], inverse, ((1,), (1,)))
    if last:
        refs[0][...] = factor
        refs[1][...] = inverse
        return
    product_kernel_body(refs[0][...], factor, *refs[1:])


def product_kernel_body(mean, factor, packed, left):
    rank = factor.shape[1]
    left_part = dot(mean, factor)
    left[...] = jnp.concatenate([left_part, left_part], axis=1)
    gram = dot(left_part, left_part, ((0,), (0,)))
    raised = dot(mean, left_part, ((0,), (0,)))
    packed[:, :rank] = raised
    packed[:, rank:] = jnp.tile(gram, (raised.shape[0] // rank, 1))


def first_kernel(mean, factor, packed, left):
    product_kernel_body(mean[...], factor[...], packed, left)


def small_call(kernel, out_shapes, *operands):
    return pl.pallas_call(
        kernel,
        out_shape=[jax.ShapeDtypeStruct(shape, f32) for shape in out_shapes],
        compiler_params=pltpu.CompilerParams(vmem_limit_bytes=32 << 20),
        cost_estimate=pl.CostEstimate(
            flops=10**9, bytes_accessed=2 << 20, transcendentals=0
        ),
    )(*operands)


def add(*values):
    total = values[0].astype(f32)
    for value in values[1:]:
        total = total + value.astype(f32)
    return total


def first_stage_kernel(
    up_y0, down_y1, below, above, up_straight, down_straight, up_crossed, down_crossed,
    sent_up, sent_down, up_up, down_down, own,
):
    first = up_y0.shape[0]
    half = up_straight.shape[1] // 2
    sent_up[:first] = add(up_y0[...], below[0]).astype(bf16)
    sent_down[:first] = add(down_y1[...], above[0]).astype(bf16)
    two = add(up_straight[0], down_crossed[0]).astype(bf16)
    up = add(up_straight[1], up_crossed[0])
    down = add(down_straight[0], down_crossed[1])
    sent_up[first : first + half] = two[:half]
    sent_down[first : first + half] = two[half:]
    sent_up[first + half :] = up[half:].astype(bf16)
    sent_down[first + half :] = down[:half].astype(bf16)
    up_up[...] = up[:half]
    down_down[...] = down[half:]
    own[...] = add(down_straight[1], up_crossed[1])


def second_stage_kernel(
    own_y1, plain_below, above_again, below_again, up_up, down_down, sent, second_up, second_down
):
    first = own_y1.shape[0]
    half = up_up.shape[0]
    sent[...] = add(own_y1[...], plain_below[0], above_again[:first]).astype(bf16)
    second_up[...] = add(up_up[...], below_again[first : first + half]).astype(bf16)
    second_down[...] = add(down_down[...], above_again[first : first + half]).astype(bf16)


def stage(kernel, shapes, planes, *operands):
    width = operands[0].shape[-1]
    columns = 256

    def by_columns(shape, plane=None):
        lead = (0,) * (len(shape) - 1)
        if plane is not None:
            shape, lead = (1,) + shape[1:], (plane,) + lead[1:]
        return pl.BlockSpec(shape[:-1] + (columns,), lambda i: lead + (i,))

    return pl.pallas_call(
        kernel,
        grid=(width // columns,),
        in_specs=[by_columns(x.shape, planes.get(at)) for at, x in enumerate(operands)],
        out_specs=[by_columns(shape) for shape, _ in shapes],
        out_shape=[jax.ShapeDtypeStruct(*shape) for shape in shapes],
        compiler_params=pltpu.CompilerParams(vmem_limit_bytes=60 << 20),
        cost_estimate=pl.CostEstimate(flops=10**7, bytes_accessed=8 << 20, transcendentals=0),
    )(*operands)


def reduce_terms(tokens_in, cotangent, spots, early_of):
    blocks = functools.partial(term_blocks, tokens_in)
    away_up = blocks(cotangent, spots, "up")
    came_up = hop(away_up, dc=1)
    away_down = blocks(after(cotangent, away_up), spots, "down")
    came_down = hop(after(away_down, came_up), dc=1)
    sent_up, up_y0, own_y1, up_straight, up_cross = blocks(
        after(cotangent, away_down), spots, "up", came_up
    )
    below = hop(sent_up, dz=1)
    up_crossed = hop(up_cross, dy=1)
    sent_down, down_y1, own_y0, down_straight, down_cross = blocks(
        after(cotangent, up_y0), spots, "down", came_down
    )
    above = hop(sent_down, dz=-1)
    down_crossed = hop(down_cross, dy=1)

    below, above, up_crossed, down_crossed = lax.optimization_barrier(
        (below, above, up_crossed, down_crossed)
    )
    half = up_straight.shape[1] // 2
    rest, width = up_straight.shape[1:]
    sent_up, sent_down, up_up, down_down, own_second = stage(
        first_stage_kernel,
        [((FIRST + rest, width), bf16)] * 2 + [((half, width), f32)] * 2 + [((rest, width), f32)],
        {2: 0, 3: 0},
        up_y0, down_y1, below, above, up_straight, down_straight, up_crossed, down_crossed,
    )
    below_again, above_again = hop(sent_up, dz=1), hop(sent_down, dz=-1)

    early = early_of(sent_up, sent_down)
    below_again, above_again, own_second = lax.optimization_barrier(
        (below_again, above_again, own_second)
    )
    sent, second_up, second_down = stage(
        second_stage_kernel,
        [((FIRST, width), bf16)] + [((half, width), bf16)] * 2,
        {1: 1},
        own_y1, below, above_again, below_again, up_up, down_down,
    )
    crossed = hop(sent, dy=1)
    crossed, last_below, last_above = lax.optimization_barrier(
        (crossed, hop(second_up, dz=1), hop(second_down, dz=-1))
    )

    second_sum = own_second + jnp.concatenate(
        [add(last_below, above_again[FIRST + half :]), add(below_again[FIRST + half :], last_above)]
    )
    first_sum = add(own_y0, below_again[:FIRST], above[1], crossed)
    return first_sum, second_sum, early


def per_device(inputs, grad_keys, local_weights, feedback, base, momentum, warm_start):
    tokens_in = inputs[0]
    cotangent = grad_keys[0]
    weights = local_weights[0]
    wide = tokens_in.shape[1]
    rep_size, fsdp_size = lax.axis_size("rep"), lax.axis_size("fsdp")
    everyone = rep_size * fsdp_size
    rows, width = weights.shape
    rank = warm_start.shape[1]
    my_rep = lax.axis_index("rep")
    block_width = base.shape[1]
    everything = ("rep", "fsdp")
    spots = all_spots()

    lane = lax.broadcasted_iota(jnp.int32, (1, width), 1)
    mine = lane // block_width == my_rep

    def early_of(*behind):
        drift = feedback[0].astype(f32) - after(weights, *behind).astype(f32)
        own_base = jnp.where(mine, jnp.tile(rep_size * base, (1, width // block_width)), 0.0)
        return scatter_sum(drift + own_base, "rep", rep_size), drift

    first_sum, second_sum, (early, drift) = reduce_terms(tokens_in, cotangent, spots, early_of)
    inner_grad = jnp.concatenate([first_sum, second_sum])
    mean = (
        early + inner_rate * scatter_sum(inner_grad.astype(bf16), "rep", rep_size)
    ) / rep_size
    moved = after(drift, mean) + inner_rate * inner_grad

    def product_shapes():
        return (width, 2 * rank), (rows // rep_size, 2 * rank)

    packed, left_part = small_call(first_kernel, product_shapes(), mean, warm_start)
    full_base = lax.all_gather(after(base, mean), "rep", axis=1, tiled=True)
    every_row = lax.all_gather(local_weights, "fsdp", axis=1, tiled=True)[0]
    grad = None
    for repeat in range(ROUNDS):
        if repeat < 2:
            grad = half_of_grad(after(cotangent, packed), every_row, repeat, grad)
        summed = gather_rows(scatter_sum(packed, everything, everyone), everything, everyone)
        summed, grad, moved = lax.optimization_barrier((summed, grad, moved))
        if repeat < ROUNDS - 1:
            packed, left_part = small_call(
                functools.partial(round_kernel, False), product_shapes(), summed, mean
            )
    left = gather_rows(after(left_part, summed), "rep", rep_size)
    factor, inverse = small_call(
        functools.partial(round_kernel, True), ((width, rank), (rank, rank)), summed
    )
    feedback_out, base_out, momentum_out = final_outputs(
        my_rep, left, inverse, factor, moved, full_base, base, momentum
    )
    return (grad[None], feedback_out[None], base_out, momentum_out, factor)


def solution(mesh):
    split = P("rep", "fsdp", None)
    shared = P("fsdp", "rep")
    return jax.shard_map(
        per_device,
        mesh=mesh,
        in_specs=(split, split, split, split, shared, shared, P()),
        out_specs=(split, split, shared, shared, P()),
        check_vma=False,
    )
```
